32 devices in a mesh: expert: 8 (over y, x, core), pair: 4 (over z).
Axes of the slice: x: 2, y: 2, z: 4, core: 2. Of those that a mesh axis runs over, the one named last changes fastest.
Arguments:
- tokens: bfloat16 [4096, 4096], P(('expert', 'pair')), may hold values from -6 to 6
- expert_ids: int32 [4096, 8], P(('expert', 'pair')), may hold values from 0 to 127, all different within a row
- route_weight: float32 [4096, 8], P(('expert', 'pair')), may hold values from 0.1 to 1
- gate_weight: bfloat16 [8, 4096, 768], P('expert'), may hold values from -0.09375 to 0.09375
- up_weight: bfloat16 [8, 4096, 768], P('expert'), may hold values from -0.09375 to 0.09375
- down_weight: bfloat16 [8, 768, 4096], P('expert'), may hold values from -0.21875 to 0.21875
Outputs:
- combined: bfloat16 [4096, 4096], P(('expert', 'pair'))
- hessian: float32 [8, 768, 768], P('expert', 'pair')
- panel: float32 [8, 768, 128], P('expert', 'pair')
The draws below stay inside these ranges and needn't reach their ends.
Inputs may be any that keep to these rules, and one draw needn't show every extreme that they name: `expert_ids`: each row names 8 different experts, and every expert is named by some row.
All inputs are finite; a program needn't handle non-finite values.
Results may differ from the reference program's by a relative error of at most 0.0057.
Values may be sent and summed in bfloat16 or wider, within the bound.
A program may use at most 128 MiB of HBM per device.

```python
import jax
import jax.numpy as jnp
from jax import lax

D = 4096
EXPERTS = 128
TOP = 8
FF = 768
PANEL = 128
TOK_DEV = 128
CAP = 16
FLIGHT = 8
TOKENS = 4096
N_EXPERT = 8
N_PAIR = 4


def levels(stream_key, extent, split, low, top_value):
    gain, own = 1.0, jax.random.fold_in(stream_key, 6)
    for dim, blocks in split:
        heights = jnp.exp(jax.random.uniform(jax.random.fold_in(own, dim), (blocks,), jnp.float32, low / len(split), top_value / len(split)))
        gain = gain * jnp.repeat(heights, extent[dim] // blocks).reshape([-1 if axis == dim else 1 for axis in range(len(extent))])
    return gain


def picks_of(rng, rows, number_of, top, lift):
    ranking = jax.random.permutation(jax.random.fold_in(rng, 1), number_of)
    pull = ranking
    for power in range(3):
        pull = pull * pull // number_of
    pull = pull * lift // number_of
    tickets = jax.random.randint(jax.random.fold_in(rng, 2), (rows, number_of), 0, 4096) + pull
    holders = jax.random.permutation(jax.random.fold_in(rng, 3), rows)[jnp.arange(number_of) % rows]
    tickets = jnp.where(jnp.arange(rows)[:, None] == holders[None, :], 1 << 14, tickets)
    merit = tickets * number_of + jnp.arange(number_of)
    return lax.top_k(merit.astype(jnp.int32), top)[1].astype(jnp.int32)


def normal_values(rng, extent, spread, most, shards=(), kind=jnp.bfloat16):
    values = jax.random.normal(rng, extent, jnp.float32) * spread
    if len(shards) > 0:
        values = levels(rng, extent, shards, -0.22, 0.18) * values
    return jnp.clip(values, min=-most, max=most).astype(kind)


def setup_inputs(seed: int = 0) -> dict:
    streams_of = jax.random.split(jax.random.key(seed), 7)
    return {
        "tokens": normal_values(streams_of[0], (TOKENS, D), 1.0, 6.0, ((0, 32),)),
        "expert_ids": picks_of(streams_of[1], TOKENS, EXPERTS, TOP, 1024),
        "route_weight": jnp.clip(0.1 + 0.9 * jax.random.uniform(streams_of[2], (TOKENS, TOP), jnp.float32) ** levels(streams_of[2], (TOKENS, TOP), ((0, 32),), -0.2, 0.2), 0.1, 1.0),
        "gate_weight": normal_values(streams_of[3], (FLIGHT, D, FF), D ** -0.5, 0.09375, ((0, 8),)),
        "up_weight": normal_values(streams_of[4], (FLIGHT, D, FF), D ** -0.5, 0.09375, ((0, 8),)),
        "down_weight": normal_values(streams_of[5], (FLIGHT, FF, D), FF ** -0.5, 0.21875, ((0, 8),)),
    }


def reference(tokens, expert_ids, route_weight, gate_weight, up_weight, down_weight):
    per_owner = EXPERTS // N_EXPERT
    sources = N_EXPERT * N_PAIR
    slot_total = sources * CAP
    grouped = expert_ids.reshape(sources, TOK_DEV, TOP)
    in_flight = grouped % per_owner == 0
    owner_of = grouped // per_owner
    columns = jnp.arange(N_EXPERT, dtype=jnp.int32)
    route_hit = (in_flight[..., None] & (owner_of[..., None] == columns)).astype(jnp.int32)
    picked = jnp.sum(route_hit, axis=2)
    before = jnp.cumsum(picked, axis=1) - picked
    kept_rows = picked * (before < CAP).astype(jnp.int32)
    rank_choice = jnp.sum(route_hit * before[:, :, None, :], axis=3)
    keep_choice = jnp.sum(route_hit * kept_rows[:, :, None, :], axis=3)
    source_ids = jnp.arange(sources, dtype=jnp.int32)[:, None, None]
    token_ids = source_ids * TOK_DEV + jnp.arange(TOK_DEV, dtype=jnp.int32)[None, :, None]
    token_ids = jnp.broadcast_to(token_ids, grouped.shape).astype(jnp.int32)
    position = owner_of * slot_total + source_ids * CAP + rank_choice
    position = jnp.where(keep_choice > 0, position, N_EXPERT * slot_total).astype(jnp.int32)
    flat_position = position.reshape(-1)
    row_table = jnp.full((N_EXPERT * slot_total,), -1, jnp.int32).at[flat_position].set(token_ids.reshape(-1), mode='drop')
    weight_table = jnp.zeros((N_EXPERT * slot_total,), jnp.float32).at[flat_position].set(route_weight.reshape(-1), mode='drop')
    hess_scale = 2.0 / (CAP * N_EXPERT * N_PAIR)
    corner_identity = jnp.eye(PANEL, dtype=jnp.float32)
    lead_identity = jnp.eye(FF, PANEL, dtype=jnp.float32)

    def one_expert(accumulated, inputs):
        row_ids, row_weights, gate_matrix, upper_matrix, down_matrix = inputs
        valid_rows = row_ids >= 0
        safe_ids = jnp.maximum(row_ids, 0).astype(jnp.int32)
        gathered = jnp.where(valid_rows[:, None], tokens[safe_ids], jnp.zeros((), tokens.dtype))
        gate_value = jnp.dot(gathered.astype(jnp.float32), gate_matrix.astype(jnp.float32), preferred_element_type=jnp.float32)
        upper_value = jnp.dot(gathered.astype(jnp.float32), upper_matrix.astype(jnp.float32), preferred_element_type=jnp.float32)
        hidden = (jax.nn.silu(gate_value) * upper_value).astype(jnp.bfloat16)
        output = jnp.dot(hidden.astype(jnp.float32), down_matrix.astype(jnp.float32), preferred_element_type=jnp.float32).astype(jnp.bfloat16)
        hessian = lax.dot_general(hidden.astype(jnp.float32), hidden.astype(jnp.float32), (((0,), (0,)), ((), ())), preferred_element_type=jnp.float32) * hess_scale
        damping = 0.01 * jnp.trace(hessian) / FF
        lower_factor = jnp.linalg.cholesky(hessian[:PANEL, :PANEL] + damping * corner_identity)
        leading = hessian[:, :PANEL] + damping * lead_identity
        panel_rows = jax.scipy.linalg.solve_triangular(lower_factor, leading.T, lower=True).T
        accumulated = accumulated.at[safe_ids].add(row_weights[:, None] * output.astype(jnp.float32))
        return (accumulated, (hessian, panel_rows))
    initial = jnp.zeros((TOKENS, D), jnp.float32)
    inputs = (row_table.reshape(N_EXPERT, slot_total), weight_table.reshape(N_EXPERT, slot_total), gate_weight, up_weight, down_weight)
    accumulated, (hessians, panels) = lax.scan(one_expert, initial, inputs)
    return (accumulated.astype(jnp.bfloat16), hessians, panels)
```

```python
import functools

import jax
import jax.numpy as jnp
from jax import lax
from jax.experimental import pallas as pl
from jax.experimental.pallas import tpu as pltpu
from jax.sharding import PartitionSpec as P

EXPERTS = 128
FF = 768
PANEL = 128
CAP = 16
CHUNKS = 4
MESH = pl.DeviceIdType.MESH
HIGHEST = lax.Precision.HIGHEST


def window_of(place, share):
    start = (place * share) // 128 * 128
    return start, place * share - start


def kernel(
    owners,
    pair_count,
    window,
    tokens_ref,
    ids_ref,
    weight_ref,
    gate_hbm,
    up_hbm,
    down_hbm,
    combined_hbm,
    hessian_hbm,
    panel_hbm,
    gate_buf,
    up_buf,
    down_buf,
    outgoing,
    arrived,
    results,
    returned,
    mixed,
    gate_acc,
    up_acc,
    hidden_all,
    squares,
    elim,
    hess_buf,
    panel_buf,
    load_sem,
    there_send,
    there_recv,
    back_send,
    back_recv,
    pair_send,
    pair_recv,
    store_sem,
):
    me = lax.axis_index("expert")
    place = lax.axis_index("pair")
    tok_count, model_width = tokens_ref.shape
    width = model_width // CHUNKS
    slots = owners * CAP
    per_owner = EXPERTS // owners
    share = FF // pair_count
    hess_scale = 2.0 / (CAP * owners * pair_count)

    def load(kind, c):
        cols = pl.ds(pl.multiple_of(c * width, 128), width)
        source, target = (
            (gate_hbm.at[0, cols, :], gate_buf.at[c]),
            (up_hbm.at[0, cols, :], up_buf.at[c]),
            (down_hbm.at[0, :, cols], down_buf.at[c]),
        )[kind]
        return pltpu.make_async_copy(source, target, load_sem.at[kind, c])

    for c in range(CHUNKS):
        load(0, c).start()
        load(1, c).start()
    for c in range(CHUNKS):
        load(2, c).start()

    barrier = pltpu.get_barrier_semaphore()
    for i in range(1, owners):
        pl.semaphore_signal(
            barrier, inc=1, device_id=(lax.rem(me + i, owners), place), device_id_type=MESH
        )
    for i in range(1, pair_count):
        pl.semaphore_signal(
            barrier, inc=1, device_id=(me, lax.rem(place + i, pair_count)), device_id_type=MESH
        )

    slot = lax.broadcasted_iota(jnp.int32, (tok_count, slots), 1)
    target = (slot // CAP) * per_owner
    picked = jnp.zeros((tok_count, slots), jnp.float32)
    slot_weight = jnp.zeros((tok_count, slots), jnp.float32)
    for k in range(ids_ref.shape[1]):
        hit = ids_ref[:, k : k + 1] == target
        picked = jnp.where(hit, 1.0, picked)
        slot_weight = jnp.where(hit, weight_ref[:, k : k + 1], slot_weight)
    earlier = lax.broadcasted_iota(jnp.int32, (tok_count, tok_count), 0) > lax.broadcasted_iota(
        jnp.int32, (tok_count, tok_count), 1
    )
    before = jnp.dot(
        earlier.astype(jnp.float32).astype(jnp.bfloat16),
        picked.astype(jnp.bfloat16),
        preferred_element_type=jnp.float32,
    )
    rank = (slot % CAP).astype(jnp.float32)
    marks = jnp.where(before == rank, picked, 0.0)
    slot_weight = slot_weight * marks
    weight_high = slot_weight.astype(jnp.bfloat16)
    weight_low = (slot_weight - weight_high.astype(jnp.float32)).astype(jnp.bfloat16)
    marks_by_slot = marks.T.astype(jnp.bfloat16)

    pl.semaphore_wait(barrier, owners + pair_count - 2)

    def there(c, i):
        peer = lax.rem(me + i, owners)
        return pltpu.make_async_remote_copy(
            src_ref=outgoing.at[c, pl.ds(pl.multiple_of(peer * CAP, CAP), CAP), :],
            dst_ref=arrived.at[c, pl.ds(pl.multiple_of(me * CAP, CAP), CAP), :],
            send_sem=there_send.at[c, i - 1],
            recv_sem=there_recv.at[c, i - 1],
            device_id=(peer, place),
            device_id_type=MESH,
        )

    def back(c, i):
        peer = lax.rem(me + i, owners)
        return pltpu.make_async_remote_copy(
            src_ref=results.at[c, pl.ds(pl.multiple_of(peer * CAP, CAP), CAP), :],
            dst_ref=returned.at[c, pl.ds(pl.multiple_of(me * CAP, CAP), CAP), :],
            send_sem=back_send.at[c, i - 1],
            recv_sem=back_recv.at[c, i - 1],
            device_id=(peer, place),
            device_id_type=MESH,
        )

    mine = pl.ds(pl.multiple_of(me * CAP, CAP), CAP)

    for c in range(CHUNKS):
        outgoing[c] = jnp.dot(
            marks_by_slot,
            tokens_ref[:, c * width : (c + 1) * width],
            preferred_element_type=jnp.float32,
        ).astype(jnp.bfloat16)
        for i in range(1, owners):
            there(c, i).start()
        arrived[c, mine, :] = outgoing[c, mine, :]

    gate_acc[...] = jnp.zeros_like(gate_acc)
    up_acc[...] = jnp.zeros_like(up_acc)

    def project(c, carry):
        load(0, c).wait()
        load(1, c).wait()
        for i in range(1, owners):
            there(c, i).wait_recv()
        rows = arrived[c]
        gate_acc[...] += jnp.dot(rows, gate_buf[c], preferred_element_type=jnp.float32)
        up_acc[...] += jnp.dot(rows, up_buf[c], preferred_element_type=jnp.float32)
        return carry

    lax.fori_loop(0, CHUNKS, project, 0)

    gate = gate_acc[...]
    hidden = (gate / (1.0 + jnp.exp(-gate)) * up_acc[...]).astype(jnp.bfloat16)
    block = pl.ds(pl.multiple_of(place * slots, CAP), slots)
    hidden_all[block, :] = hidden
    square = hidden.astype(jnp.float32)
    square = jnp.sum((square * square).reshape(slots // 8, 8, FF), axis=0)
    total = square[:, 0:128]
    for part in range(1, FF // 128):
        total = total + square[:, part * 128 : (part + 1) * 128]
    squares[place] = total

    def shared(kind, i):
        ref = (
            hidden_all.at[block, 0:PANEL],
            squares.at[place],
            hidden_all.at[block, PANEL:FF],
        )[kind]
        return pltpu.make_async_remote_copy(
            src_ref=ref,
            dst_ref=ref,
            send_sem=pair_send.at[kind, i - 1],
            recv_sem=pair_recv.at[kind, i - 1],
            device_id=(me, lax.rem(place + i, pair_count)),
            device_id_type=MESH,
        )

    for kind in range(3):
        for i in range(1, pair_count):
            shared(kind, i).start()

    def project_down(c, carry):
        load(2, c).wait()
        results[c] = jnp.dot(
            hidden_all[block, :], down_buf[c], preferred_element_type=jnp.float32
        ).astype(jnp.bfloat16)
        for i in range(1, owners):
            back(c, i).start()
        returned[c, mine, :] = results[c, mine, :]
        return carry

    lax.fori_loop(0, CHUNKS, project_down, 0)

    for i in range(1, pair_count):
        shared(0, i).wait_recv()
        shared(1, i).wait_recv()
    damping = jnp.sum(jnp.sum(squares[...], axis=0), axis=0, keepdims=True)
    damping = jnp.sum(damping, axis=1, keepdims=True) * (0.01 * hess_scale / FF)
    row_ids = lax.broadcasted_iota(jnp.int32, (PANEL, PANEL), 0)
    column_ids = lax.broadcasted_iota(jnp.int32, (PANEL, PANEL), 1)
    diagonal = row_ids == column_ids
    lead = hidden_all[:, 0:PANEL]
    corner = lax.dot_general(
        lead, lead, (((0,), (0,)), ((), ())), preferred_element_type=jnp.float32
    )
    elim[...] = corner * hess_scale + jnp.where(diagonal, damping, 0.0)
    row_number = lax.broadcasted_iota(jnp.int32, (PANEL, 1), 0)
    lane_number = lax.broadcasted_iota(jnp.int32, (1, PANEL), 1)

    def eliminate(j, carry):
        rest = elim[...]
        row = elim[pl.ds(j, 1), :]
        lane = lane_number == j
        pivot = jnp.sum(jnp.where(lane, row, 0.0), axis=1, keepdims=True)
        column = jnp.sum(jnp.where(lane, rest, 0.0), axis=1, keepdims=True)
        below = row_number > j
        factor = jnp.where(below, column * (1.0 / pivot), 0.0)
        elim[...] = jnp.where(lane, jnp.where(below, -factor, column), rest - factor * row)
        return carry

    lax.fori_loop(0, PANEL, eliminate, 0)
    done = elim[...]
    pivots = jnp.sum(jnp.where(diagonal, done, 0.0), axis=1, keepdims=True)
    inverse = jnp.where(row_ids > column_ids, done, jnp.where(diagonal, 1.0, 0.0))
    inverse = inverse * lax.rsqrt(pivots)

    for i in range(1, pair_count):
        shared(2, i).wait_recv()
    start, offset = window_of(place, share)
    hess_buf[...] = (
        lax.dot_general(
            hidden_all[:, pl.ds(pl.multiple_of(start, 128), window)],
            hidden_all[...],
            (((0,), (0,)), ((), ())),
            preferred_element_type=jnp.float32,
        )
        * hess_scale
    )
    my_rows = pl.ds(pl.multiple_of(offset, 8), share)
    store_hessian = pltpu.make_async_copy(
        hess_buf.at[my_rows, :], hessian_hbm.at[0], store_sem.at[CHUNKS]
    )
    store_hessian.start()
    own_ids = place * share + lax.broadcasted_iota(jnp.int32, (share, PANEL), 0)
    own_columns = lax.broadcasted_iota(jnp.int32, (share, PANEL), 1)
    leading = hess_buf[my_rows, 0:PANEL] + jnp.where(own_ids == own_columns, damping, 0.0)
    panel_buf[...] = lax.dot_general(
        leading,
        inverse,
        (((1,), (1,)), ((), ())),
        precision=HIGHEST,
        preferred_element_type=jnp.float32,
    )
    store_panel = pltpu.make_async_copy(panel_buf, panel_hbm.at[0], store_sem.at[CHUNKS + 1])
    store_panel.start()

    def store(c):
        cols = pl.ds(pl.multiple_of(c * width, 128), width)
        return pltpu.make_async_copy(mixed.at[c], combined_hbm.at[:, cols], store_sem.at[c])

    for c in range(CHUNKS):
        for i in range(1, owners):
            back(c, i).wait_recv()
        rows = returned[c]
        mixed[c] = (
            jnp.dot(weight_high, rows, preferred_element_type=jnp.float32)
            + jnp.dot(weight_low, rows, preferred_element_type=jnp.float32)
        ).astype(jnp.bfloat16)
        store(c).start()

    for c in range(CHUNKS):
        for i in range(1, owners):
            there(c, i).wait_send()
            back(c, i).wait_send()
    for i in range(1, pair_count):
        for kind in range(3):
            shared(kind, i).wait_send()
    store_hessian.wait()
    store_panel.wait()
    for c in range(CHUNKS):
        store(c).wait()


def per_device(
    owners, pair_count, tokens, expert_ids, route_weight, gate_weight, up_weight, down_weight
):
    tok_count, model_width = tokens.shape
    width = model_width // CHUNKS
    slots = owners * CAP
    share = FF // pair_count
    reach = max(window_of(p, share)[1] for p in range(pair_count)) + share
    window = -(-reach // 128) * 128
    vmem = pl.BlockSpec(memory_space=pltpu.VMEM)
    hbm = pl.BlockSpec(memory_space=pl.ANY)
    bf16, f32 = jnp.bfloat16, jnp.float32
    dma = pltpu.SemaphoreType.DMA
    return pl.pallas_call(
        functools.partial(kernel, owners, pair_count, window),
        out_shape=(
            jax.ShapeDtypeStruct((tok_count, model_width), bf16),
            jax.ShapeDtypeStruct((1, share, FF), f32),
            jax.ShapeDtypeStruct((1, share, PANEL), f32),
        ),
        in_specs=[vmem, vmem, vmem, hbm, hbm, hbm],
        out_specs=(hbm, hbm, hbm),
        scratch_shapes=[
            pltpu.VMEM((CHUNKS, width, FF), bf16),
            pltpu.VMEM((CHUNKS, width, FF), bf16),
            pltpu.VMEM((CHUNKS, FF, width), bf16),
            pltpu.VMEM((CHUNKS, slots, width), bf16),
            pltpu.VMEM((CHUNKS, slots, width), bf16),
            pltpu.VMEM((CHUNKS, slots, width), bf16),
            pltpu.VMEM((CHUNKS, slots, width), bf16),
            pltpu.VMEM((CHUNKS, tok_count, width), bf16),
            pltpu.VMEM((slots, FF), f32),
            pltpu.VMEM((slots, FF), f32),
            pltpu.VMEM((pair_count * slots, FF), bf16),
            pltpu.VMEM((pair_count, 8, 128), f32),
            pltpu.VMEM((PANEL, PANEL), f32),
            pltpu.VMEM((window, FF), f32),
            pltpu.VMEM((share, PANEL), f32),
            dma((3, CHUNKS)),
            dma((CHUNKS, owners - 1)),
            dma((CHUNKS, owners - 1)),
            dma((CHUNKS, owners - 1)),
            dma((CHUNKS, owners - 1)),
            dma((3, pair_count - 1)),
            dma((3, pair_count - 1)),
            dma((CHUNKS + 2,)),
        ],
        compiler_params=pltpu.CompilerParams(
            collective_id=0, has_side_effects=True, vmem_limit_bytes=56 * 1024 * 1024
        ),
        cost_estimate=pl.CostEstimate(
            flops=2 * slots * model_width * FF * 3,
            bytes_accessed=3 * 2 * model_width * FF,
            transcendentals=slots * FF,
        ),
        name="experts",
    )(tokens, expert_ids, route_weight, gate_weight, up_weight, down_weight)


def solution(mesh):
    in_specs = (
        P(("expert", "pair"), None),
        P(("expert", "pair"), None),
        P(("expert", "pair"), None),
        P("expert", None, None),
        P("expert", None, None),
        P("expert", None, None),
    )
    out_specs = (P(("expert", "pair"), None), P("expert", "pair", None), P("expert", "pair", None))
    return jax.shard_map(
        functools.partial(per_device, mesh.shape["expert"], mesh.shape["pair"]),
        mesh=mesh,
        in_specs=in_specs,
        out_specs=out_specs,
        check_vma=False,
    )
```

```python
import functools

import jax
import jax.numpy as jnp
from jax import lax
from jax.experimental import pallas as pl
from jax.experimental.pallas import tpu as pltpu
from jax.sharding import PartitionSpec as P

EXPERTS = 128
FF = 768
PANEL = 128
CAP = 16
CHUNKS = 4
MESH = pl.DeviceIdType.MESH
HIGHEST = lax.Precision.HIGHEST


def window_of(place, share):
    start = (place * share) // 128 * 128
    return start, place * share - start


def kernel(
    owners,
    pair_count,
    window,
    tokens_ref,
    ids_ref,
    weight_ref,
    gate_hbm,
    up_hbm,
    down_hbm,
    returned,
    mix_hbm,
    hessian_hbm,
    panel_hbm,
    gate_buf,
    up_buf,
    down_buf,
    outgoing,
    arrived,
    results,
    mix_buf,
    gate_acc,
    up_acc,
    hidden_all,
    squares,
    elim,
    hess_buf,
    panel_buf,
    load_sem,
    there_send,
    there_recv,
    back_send,
    back_recv,
    pair_send,
    pair_recv,
    pass_send,
    pass_recv,
    store_sem,
):
    me = lax.axis_index("expert")
    place = lax.axis_index("pair")
    tok_count, model_width = tokens_ref.shape
    width = model_width // CHUNKS
    slots = owners * CAP
    per_owner = EXPERTS // owners
    share = FF // pair_count
    hess_scale = 2.0 / (CAP * owners * pair_count)

    def load(kind, c):
        cols = pl.ds(pl.multiple_of(c * width, 128), width)
        source, target = (
            (gate_hbm.at[0, cols, :], gate_buf.at[c]),
            (up_hbm.at[0, cols, :], up_buf.at[c]),
            (down_hbm.at[0, :, cols], down_buf.at[c]),
        )[kind]
        return pltpu.make_async_copy(source, target, load_sem.at[kind, c])

    for c in range(CHUNKS):
        load(0, c).start()
        load(1, c).start()
    for c in range(CHUNKS):
        load(2, c).start()

    barrier = pltpu.get_barrier_semaphore()
    for i in range(1, owners):
        pl.semaphore_signal(
            barrier, inc=1, device_id=(lax.rem(me + i, owners), place), device_id_type=MESH
        )
    for i in range(1, pair_count):
        pl.semaphore_signal(
            barrier, inc=1, device_id=(me, lax.rem(place + i, pair_count)), device_id_type=MESH
        )

    slot = lax.broadcasted_iota(jnp.int32, (slots, tok_count), 0)
    target = (slot // CAP) * per_owner
    picked = jnp.zeros((slots, tok_count), jnp.float32)
    slot_weight = jnp.zeros((slots, tok_count), jnp.float32)
    for k in range(ids_ref.shape[0]):
        hit = ids_ref[k : k + 1, :] == target
        picked = jnp.where(hit, 1.0, picked)
        slot_weight = jnp.where(hit, weight_ref[k : k + 1, :], slot_weight)
    earlier = lax.broadcasted_iota(jnp.int32, (tok_count, tok_count), 0) < lax.broadcasted_iota(
        jnp.int32, (tok_count, tok_count), 1
    )
    before = jnp.dot(
        picked.astype(jnp.bfloat16),
        earlier.astype(jnp.float32).astype(jnp.bfloat16),
        preferred_element_type=jnp.float32,
    )
    rank = (slot % CAP).astype(jnp.float32)
    marks = jnp.where(before == rank, picked, 0.0)
    marks_by_slot = marks.astype(jnp.bfloat16)

    pl.semaphore_wait(barrier, owners + pair_count - 2)

    def there(c, i):
        peer = lax.rem(me + i, owners)
        return pltpu.make_async_remote_copy(
            src_ref=outgoing.at[c, pl.ds(pl.multiple_of(peer * CAP, CAP), CAP), :],
            dst_ref=arrived.at[c, pl.ds(pl.multiple_of(me * CAP, CAP), CAP), :],
            send_sem=there_send.at[c, i - 1],
            recv_sem=there_recv.at[c, i - 1],
            device_id=(peer, place),
            device_id_type=MESH,
        )

    def back(c, i):
        peer = lax.rem(me + i, owners)
        return pltpu.make_async_remote_copy(
            src_ref=results.at[c, pl.ds(pl.multiple_of(peer * CAP, CAP), CAP), :],
            dst_ref=returned.at[c, pl.ds(pl.multiple_of(me * CAP, CAP), CAP), :],
            send_sem=back_send.at[c, i - 1],
            recv_sem=back_recv.at[c, i - 1],
            device_id=(peer, place),
            device_id_type=MESH,
        )

    def keep(c):
        return pltpu.make_async_copy(
            results.at[c, mine, :], returned.at[c, mine, :], store_sem.at[c]
        )

    mine = pl.ds(pl.multiple_of(me * CAP, CAP), CAP)

    for c in range(CHUNKS):
        outgoing[c] = jnp.dot(
            marks_by_slot,
            tokens_ref[:, c * width : (c + 1) * width],
            preferred_element_type=jnp.float32,
        ).astype(jnp.bfloat16)
        for i in range(1, owners):
            there(c, i).start()
        arrived[c, mine, :] = outgoing[c, mine, :]

    weights = (slot_weight * marks).T
    weight_high = weights.astype(jnp.bfloat16)
    mix_buf[0] = weight_high
    mix_buf[1] = (weights - weight_high.astype(jnp.float32)).astype(jnp.bfloat16)
    store_mix = pltpu.make_async_copy(mix_buf, mix_hbm, store_sem.at[CHUNKS + 2])
    store_mix.start()

    gate_acc[...] = jnp.zeros_like(gate_acc)
    up_acc[...] = jnp.zeros_like(up_acc)

    def project(c, carry):
        load(0, c).wait()
        load(1, c).wait()
        for i in range(1, owners):
            there(c, i).wait_recv()
        rows = arrived[c]
        gate_acc[...] += jnp.dot(rows, gate_buf[c], preferred_element_type=jnp.float32)
        up_acc[...] += jnp.dot(rows, up_buf[c], preferred_element_type=jnp.float32)
        return carry

    lax.fori_loop(0, CHUNKS, project, 0)

    gate = gate_acc[...]
    hidden = (gate / (1.0 + jnp.exp(-gate)) * up_acc[...]).astype(jnp.bfloat16)
    block = pl.ds(pl.multiple_of(place * slots, CAP), slots)
    hidden_all[block, :] = hidden
    square = hidden.astype(jnp.float32)
    square = jnp.sum((square * square).reshape(slots // 8, 8, FF), axis=0)
    total = square[:, 0:128]
    for part in range(1, FF // 128):
        total = total + square[:, part * 128 : (part + 1) * 128]
    squares[place] = total

    def shared(kind, i):
        ref = (
            hidden_all.at[block, 0:PANEL],
            squares.at[place],
        )[kind]
        return pltpu.make_async_remote_copy(
            src_ref=ref,
            dst_ref=ref,
            send_sem=pair_send.at[kind, i - 1],
            recv_sem=pair_recv.at[kind, i - 1],
            device_id=(me, lax.rem(place + i, pair_count)),
            device_id_type=MESH,
        )

    def passing(step, side, number):
        toward = (1, -1)[side]
        ref = hidden_all.at[pl.ds(pl.multiple_of(number * slots, CAP), slots), PANEL:FF]
        return pltpu.make_async_remote_copy(
            src_ref=ref,
            dst_ref=ref,
            send_sem=pass_send.at[side, step - 1],
            recv_sem=pass_recv.at[side, step - 1],
            device_id=(me, lax.rem(place + toward + pair_count, pair_count)),
            device_id_type=MESH,
        )

    def each_send(step, action):
        @pl.when(jnp.logical_and(place >= step - 1, place < pair_count - 1))
        def _():
            action(passing(step, 0, place - step + 1))

        @pl.when(jnp.logical_and(place <= pair_count - step, place > 0))
        def _():
            action(passing(step, 1, place + step - 1))

    def receive(step):
        @pl.when(place >= step)
        def _():
            passing(step, 0, place - step).wait_recv()

        @pl.when(place < pair_count - step)
        def _():
            passing(step, 1, place + step).wait_recv()

    for kind in range(2):
        for i in range(1, pair_count):
            shared(kind, i).start()
    each_send(1, lambda copy: copy.start())

    def project_down(c, carry):
        load(2, c).wait()
        results[c] = jnp.dot(
            hidden_all[block, :], down_buf[c], preferred_element_type=jnp.float32
        ).astype(jnp.bfloat16)
        for i in range(1, owners):
            back(c, i).start()
        keep(c).start()
        return carry

    lax.fori_loop(0, CHUNKS, project_down, 0)

    for i in range(1, pair_count):
        shared(0, i).wait_recv()
        shared(1, i).wait_recv()
    damping = jnp.sum(jnp.sum(squares[...], axis=0), axis=0, keepdims=True)
    damping = jnp.sum(damping, axis=1, keepdims=True) * (0.01 * hess_scale / FF)
    row_ids = lax.broadcasted_iota(jnp.int32, (PANEL, PANEL), 0)
    column_ids = lax.broadcasted_iota(jnp.int32, (PANEL, PANEL), 1)
    diagonal = row_ids == column_ids
    lead = hidden_all[:, 0:PANEL]
    corner = lax.dot_general(
        lead, lead, (((0,), (0,)), ((), ())), preferred_element_type=jnp.float32
    )
    elim[...] = corner * hess_scale + jnp.where(diagonal, damping, 0.0)
    row_number = lax.broadcasted_iota(jnp.int32, (PANEL, 1), 0)
    lane_number = lax.broadcasted_iota(jnp.int32, (1, PANEL), 1)

    def eliminate(pair, carry):
        j = 2 * pair
        rest = elim[...]
        row0 = elim[pl.ds(j, 1), :]
        row1 = elim[pl.ds(j + 1, 1), :]
        lane0 = lane_number == j
        lane1 = lane_number == j + 1
        pivot0 = jnp.sum(jnp.where(lane0, row0, 0.0), axis=1, keepdims=True)
        cross = jnp.sum(jnp.where(lane1, row0, 0.0), axis=1, keepdims=True)
        pivot1 = jnp.sum(jnp.where(lane1, row1, 0.0), axis=1, keepdims=True)
        column0 = jnp.sum(jnp.where(lane0, rest, 0.0), axis=1, keepdims=True)
        column1 = jnp.sum(jnp.where(lane1, rest, 0.0), axis=1, keepdims=True)
        below = row_number > j + 1
        scale0 = 1.0 / pivot0
        ratio = cross * scale0
        pivot1 = pivot1 - ratio * cross
        scale1 = 1.0 / pivot1
        factor0 = jnp.where(below, column0 * scale0, 0.0)
        factor1 = jnp.where(below, (column1 - factor0 * cross) * scale1, 0.0)
        next1 = jnp.where(lane0, -ratio, row1 - ratio * row0)
        take0 = jnp.where(lane0, 1.0, jnp.where(lane1, 0.0, row0))
        take1 = jnp.where(lane1, 1.0, next1)
        cleared = jnp.logical_and(jnp.logical_or(lane0, lane1), below)
        elim[...] = jnp.where(cleared, 0.0, rest) - factor0 * take0 - factor1 * take1
        elim[pl.ds(j + 1, 1), :] = jnp.where(lane1, pivot1, next1)
        return carry

    first = 0
    for step in range(1, pair_count):
        last = PANEL // 2 if step == pair_count - 1 else min(PANEL // 2, 28 * step - 12)
        lax.fori_loop(first, last, eliminate, 0)
        first = last
        if step < pair_count - 1:
            receive(step)
            each_send(step + 1, lambda copy: copy.start())
    done = elim[...]
    pivots = jnp.sum(jnp.where(diagonal, done, 0.0), axis=1, keepdims=True)
    inverse = jnp.where(row_ids > column_ids, done, jnp.where(diagonal, 1.0, 0.0))
    inverse = inverse * lax.rsqrt(pivots)

    receive(pair_count - 1)
    start, offset = window_of(place, share)
    hess_buf[...] = (
        lax.dot_general(
            hidden_all[:, pl.ds(pl.multiple_of(start, 128), window)],
            hidden_all[...],
            (((0,), (0,)), ((), ())),
            preferred_element_type=jnp.float32,
        )
        * hess_scale
    )
    my_rows = pl.ds(pl.multiple_of(offset, 8), share)
    store_hessian = pltpu.make_async_copy(
        hess_buf.at[my_rows, :], hessian_hbm.at[0], store_sem.at[CHUNKS]
    )
    store_hessian.start()
    own_ids = place * share + lax.broadcasted_iota(jnp.int32, (share, PANEL), 0)
    own_columns = lax.broadcasted_iota(jnp.int32, (share, PANEL), 1)
    leading = hess_buf[my_rows, 0:PANEL] + jnp.where(own_ids == own_columns, damping, 0.0)
    panel_buf[...] = lax.dot_general(
        leading,
        inverse,
        (((1,), (1,)), ((), ())),
        precision=HIGHEST,
        preferred_element_type=jnp.float32,
    )
    store_panel = pltpu.make_async_copy(panel_buf, panel_hbm.at[0], store_sem.at[CHUNKS + 1])
    store_panel.start()

    for c in range(CHUNKS):
        for i in range(1, owners):
            back(c, i).wait_recv()
        keep(c).wait()
    for c in range(CHUNKS):
        for i in range(1, owners):
            there(c, i).wait_send()
            back(c, i).wait_send()
    for i in range(1, pair_count):
        for kind in range(2):
            shared(kind, i).wait_send()
    store_hessian.wait()
    for step in range(1, pair_count):
        each_send(step, lambda copy: copy.wait_send())
    store_panel.wait()
    store_mix.wait()


def combine(returned_ref, mix_ref, hessian_ref, panel_ref, combined_ref, hessian_out, panel_out):
    rows = returned_ref[0]
    combined_ref[...] = (
        jnp.dot(mix_ref[0], rows, preferred_element_type=jnp.float32)
        + jnp.dot(mix_ref[1], rows, preferred_element_type=jnp.float32)
    ).astype(jnp.bfloat16)
    hessian_out[...] = hessian_ref[...]
    panel_out[...] = panel_ref[...]


def per_device(
    owners, pair_count, tokens, expert_ids, route_weight, gate_weight, up_weight, down_weight
):
    tok_count, model_width = tokens.shape
    width = model_width // CHUNKS
    slots = owners * CAP
    share = FF // pair_count
    reach = max(window_of(p, share)[1] for p in range(pair_count)) + share
    window = -(-reach // 128) * 128
    vmem = pl.BlockSpec(memory_space=pltpu.VMEM)
    hbm = pl.BlockSpec(memory_space=pl.ANY)
    bf16, f32 = jnp.bfloat16, jnp.float32
    dma = pltpu.SemaphoreType.DMA
    returned, mix, hessian, panel = pl.pallas_call(
        functools.partial(kernel, owners, pair_count, window),
        out_shape=(
            jax.ShapeDtypeStruct((CHUNKS, slots, width), bf16),
            jax.ShapeDtypeStruct((2, tok_count, slots), bf16),
            jax.ShapeDtypeStruct((1, share, FF), f32),
            jax.ShapeDtypeStruct((1, share, PANEL), f32),
        ),
        in_specs=[vmem, vmem, vmem, hbm, hbm, hbm],
        out_specs=(hbm, hbm, hbm, hbm),
        scratch_shapes=[
            pltpu.VMEM((CHUNKS, width, FF), bf16),
            pltpu.VMEM((CHUNKS, width, FF), bf16),
            pltpu.VMEM((CHUNKS, FF, width), bf16),
            pltpu.VMEM((CHUNKS, slots, width), bf16),
            pltpu.VMEM((CHUNKS, slots, width), bf16),
            pltpu.VMEM((CHUNKS, slots, width), bf16),
            pltpu.VMEM((2, tok_count, slots), bf16),
            pltpu.VMEM((slots, FF), f32),
            pltpu.VMEM((slots, FF), f32),
            pltpu.VMEM((pair_count * slots, FF), bf16),
            pltpu.VMEM((pair_count, 8, 128), f32),
            pltpu.VMEM((PANEL, PANEL), f32),
            pltpu.VMEM((window, FF), f32),
            pltpu.VMEM((share, PANEL), f32),
            dma((3, CHUNKS)),
            dma((CHUNKS, owners - 1)),
            dma((CHUNKS, owners - 1)),
            dma((CHUNKS, owners - 1)),
            dma((CHUNKS, owners - 1)),
            dma((2, pair_count - 1)),
            dma((2, pair_count - 1)),
            dma((2, pair_count - 1)),
            dma((2, pair_count - 1)),
            dma((CHUNKS + 3,)),
        ],
        compiler_params=pltpu.CompilerParams(
            collective_id=0, has_side_effects=True, vmem_limit_bytes=56 * 1024 * 1024
        ),
        cost_estimate=pl.CostEstimate(
            flops=2 * slots * model_width * FF * 3,
            bytes_accessed=3 * 2 * model_width * FF,
            transcendentals=slots * FF,
        ),
        name="experts",
    )(tokens, expert_ids.T, route_weight.T, gate_weight, up_weight, down_weight)
    strip = share // CHUNKS
    hessian_spec = pl.BlockSpec((1, strip, FF), lambda c: (0, c, 0))
    panel_spec = pl.BlockSpec((1, strip, PANEL), lambda c: (0, c, 0))
    return pl.pallas_call(
        combine,
        grid=(CHUNKS,),
        out_shape=(
            jax.ShapeDtypeStruct((tok_count, model_width), bf16),
            jax.ShapeDtypeStruct((1, share, FF), f32),
            jax.ShapeDtypeStruct((1, share, PANEL), f32),
        ),
        in_specs=[
            pl.BlockSpec((1, slots, width), lambda c: (c, 0, 0)),
            pl.BlockSpec((2, tok_count, slots), lambda c: (0, 0, 0)),
            hessian_spec,
            panel_spec,
        ],
        out_specs=(
            pl.BlockSpec((tok_count, width), lambda c: (0, c)),
            hessian_spec,
            panel_spec,
        ),
        cost_estimate=pl.CostEstimate(
            flops=4 * tok_count * slots * model_width,
            bytes_accessed=4 * slots * model_width + 8 * share * (FF + PANEL),
            transcendentals=0,
        ),
        name="combine",
    )(returned, mix, hessian, panel)


def solution(mesh):
    in_specs = (
        P(("expert", "pair"), None),
        P(("expert", "pair"), None),
        P(("expert", "pair"), None),
        P("expert", None, None),
        P("expert", None, None),
        P("expert", None, None),
    )
    out_specs = (P(("expert", "pair"), None), P("expert", "pair", None), P("expert", "pair", None))
    return jax.shard_map(
        functools.partial(per_device, mesh.shape["expert"], mesh.shape["pair"]),
        mesh=mesh,
        in_specs=in_specs,
        out_specs=out_specs,
        check_vma=False,
    )
```

```python
import functools

import jax
import jax.numpy as jnp
from jax import lax
from jax.experimental import pallas as pl
from jax.experimental.pallas import tpu as pltpu
from jax.sharding import PartitionSpec as P

EXPERTS = 128
FF = 768
PANEL = 128
CAP = 16
CHUNKS = 4
GROUP = 4
MESH = pl.DeviceIdType.MESH
HIGHEST = lax.Precision.HIGHEST


def window_of(place, share):
    start = (place * share) // 128 * 128
    return start, place * share - start


def kernel(
    owners,
    pair_count,
    window,
    tokens_ref,
    ids_ref,
    weight_ref,
    gate_hbm,
    up_hbm,
    down_hbm,
    returned,
    mix_hbm,
    hessian_hbm,
    panel_hbm,
    gate_buf,
    up_buf,
    down_buf,
    outgoing,
    arrived,
    results,
    mix_buf,
    gate_acc,
    up_acc,
    hidden_all,
    squares,
    elim,
    hess_buf,
    panel_buf,
    load_sem,
    there_send,
    there_recv,
    back_send,
    back_recv,
    pair_send,
    pair_recv,
    pass_send,
    pass_recv,
    store_sem,
):
    me = lax.axis_index("expert")
    place = lax.axis_index("pair")
    tok_count, model_width = tokens_ref.shape
    width = model_width // CHUNKS
    slots = owners * CAP
    per_owner = EXPERTS // owners
    share = FF // pair_count
    hess_scale = 2.0 / (CAP * owners * pair_count)

    def load(kind, c):
        cols = pl.ds(pl.multiple_of(c * width, 128), width)
        source, target = (
            (gate_hbm.at[0, cols, :], gate_buf.at[c]),
            (up_hbm.at[0, cols, :], up_buf.at[c]),
            (down_hbm.at[0, :, cols], down_buf.at[c]),
        )[kind]
        return pltpu.make_async_copy(source, target, load_sem.at[kind, c])

    for c in range(CHUNKS):
        load(0, c).start()
        load(1, c).start()
    for c in range(CHUNKS):
        load(2, c).start()

    barrier = pltpu.get_barrier_semaphore()
    for i in range(1, owners):
        pl.semaphore_signal(
            barrier, inc=1, device_id=(lax.rem(me + i, owners), place), device_id_type=MESH
        )
    for i in range(1, pair_count):
        pl.semaphore_signal(
            barrier, inc=1, device_id=(me, lax.rem(place + i, pair_count)), device_id_type=MESH
        )

    slot = lax.broadcasted_iota(jnp.int32, (slots, tok_count), 0)
    target = (slot // CAP) * per_owner
    picked = jnp.zeros((slots, tok_count), jnp.float32)
    slot_weight = jnp.zeros((slots, tok_count), jnp.float32)
    for k in range(ids_ref.shape[0]):
        hit = ids_ref[k : k + 1, :] == target
        picked = jnp.where(hit, 1.0, picked)
        slot_weight = jnp.where(hit, weight_ref[k : k + 1, :], slot_weight)
    earlier = lax.broadcasted_iota(jnp.int32, (tok_count, tok_count), 0) < lax.broadcasted_iota(
        jnp.int32, (tok_count, tok_count), 1
    )
    before = jnp.dot(
        picked.astype(jnp.bfloat16),
        earlier.astype(jnp.float32).astype(jnp.bfloat16),
        preferred_element_type=jnp.float32,
    )
    rank = (slot % CAP).astype(jnp.float32)
    marks = jnp.where(before == rank, picked, 0.0)
    marks_by_slot = marks.astype(jnp.bfloat16)

    pl.semaphore_wait(barrier, owners + pair_count - 2)

    def there(c, i):
        peer = lax.rem(me + i, owners)
        return pltpu.make_async_remote_copy(
            src_ref=outgoing.at[c, pl.ds(pl.multiple_of(peer * CAP, CAP), CAP), :],
            dst_ref=arrived.at[c, pl.ds(pl.multiple_of(me * CAP, CAP), CAP), :],
            send_sem=there_send.at[c, i - 1],
            recv_sem=there_recv.at[c, i - 1],
            device_id=(peer, place),
            device_id_type=MESH,
        )

    def back(c, i):
        peer = lax.rem(me + i, owners)
        return pltpu.make_async_remote_copy(
            src_ref=results.at[c, pl.ds(pl.multiple_of(peer * CAP, CAP), CAP), :],
            dst_ref=returned.at[c, pl.ds(pl.multiple_of(me * CAP, CAP), CAP), :],
            send_sem=back_send.at[c, i - 1],
            recv_sem=back_recv.at[c, i - 1],
            device_id=(peer, place),
            device_id_type=MESH,
        )

    def keep(c):
        return pltpu.make_async_copy(
            results.at[c, mine, :], returned.at[c, mine, :], store_sem.at[c]
        )

    mine = pl.ds(pl.multiple_of(me * CAP, CAP), CAP)

    for c in range(CHUNKS):
        outgoing[c] = jnp.dot(
            marks_by_slot,
            tokens_ref[:, c * width : (c + 1) * width],
            preferred_element_type=jnp.float32,
        ).astype(jnp.bfloat16)
        for i in range(1, owners):
            there(c, i).start()
        arrived[c, mine, :] = outgoing[c, mine, :]

    weights = (slot_weight * marks).T
    weight_high = weights.astype(jnp.bfloat16)
    mix_buf[0] = weight_high
    mix_buf[1] = (weights - weight_high.astype(jnp.float32)).astype(jnp.bfloat16)
    store_mix = pltpu.make_async_copy(mix_buf, mix_hbm, store_sem.at[CHUNKS + 2])
    store_mix.start()

    gate_acc[...] = jnp.zeros_like(gate_acc)
    up_acc[...] = jnp.zeros_like(up_acc)

    def project(c, carry):
        load(0, c).wait()
        load(1, c).wait()
        for i in range(1, owners):
            there(c, i).wait_recv()
        rows = arrived[c]
        gate_acc[...] += jnp.dot(rows, gate_buf[c], preferred_element_type=jnp.float32)
        up_acc[...] += jnp.dot(rows, up_buf[c], preferred_element_type=jnp.float32)
        return carry

    lax.fori_loop(0, CHUNKS, project, 0)

    gate = gate_acc[...]
    hidden = (gate / (1.0 + jnp.exp(-gate)) * up_acc[...]).astype(jnp.bfloat16)
    block = pl.ds(pl.multiple_of(place * slots, CAP), slots)
    hidden_all[block, :] = hidden
    square = hidden.astype(jnp.float32)
    square = jnp.sum((square * square).reshape(slots // 8, 8, FF), axis=0)
    total = square[:, 0:128]
    for part in range(1, FF // 128):
        total = total + square[:, part * 128 : (part + 1) * 128]
    squares[place] = total

    def shared(kind, i):
        ref = (
            hidden_all.at[block, 0:PANEL],
            squares.at[place],
        )[kind]
        return pltpu.make_async_remote_copy(
            src_ref=ref,
            dst_ref=ref,
            send_sem=pair_send.at[kind, i - 1],
            recv_sem=pair_recv.at[kind, i - 1],
            device_id=(me, lax.rem(place + i, pair_count)),
            device_id_type=MESH,
        )

    def passing(step, side, number):
        toward = (1, -1)[side]
        ref = hidden_all.at[pl.ds(pl.multiple_of(number * slots, CAP), slots), PANEL:FF]
        return pltpu.make_async_remote_copy(
            src_ref=ref,
            dst_ref=ref,
            send_sem=pass_send.at[side, step - 1],
            recv_sem=pass_recv.at[side, step - 1],
            device_id=(me, lax.rem(place + toward + pair_count, pair_count)),
            device_id_type=MESH,
        )

    def each_send(step, action):
        @pl.when(jnp.logical_and(place >= step - 1, place < pair_count - 1))
        def _():
            action(passing(step, 0, place - step + 1))

        @pl.when(jnp.logical_and(place <= pair_count - step, place > 0))
        def _():
            action(passing(step, 1, place + step - 1))

    def receive(step):
        @pl.when(place >= step)
        def _():
            passing(step, 0, place - step).wait_recv()

        @pl.when(place < pair_count - step)
        def _():
            passing(step, 1, place + step).wait_recv()

    for kind in range(2):
        for i in range(1, pair_count):
            shared(kind, i).start()
    each_send(1, lambda copy: copy.start())

    def project_down(c, carry):
        load(2, c).wait()
        results[c] = jnp.dot(
            hidden_all[block, :], down_buf[c], preferred_element_type=jnp.float32
        ).astype(jnp.bfloat16)
        for i in range(1, owners):
            back(c, i).start()
        keep(c).start()
        return carry

    lax.fori_loop(0, CHUNKS, project_down, 0)

    for i in range(1, pair_count):
        shared(0, i).wait_recv()
        shared(1, i).wait_recv()
    damping = jnp.sum(jnp.sum(squares[...], axis=0), axis=0, keepdims=True)
    damping = jnp.sum(damping, axis=1, keepdims=True) * (0.01 * hess_scale / FF)
    row_ids = lax.broadcasted_iota(jnp.int32, (PANEL, PANEL), 0)
    column_ids = lax.broadcasted_iota(jnp.int32, (PANEL, PANEL), 1)
    diagonal = row_ids == column_ids
    lead = hidden_all[:, 0:PANEL]
    corner = lax.dot_general(
        lead, lead, (((0,), (0,)), ((), ())), preferred_element_type=jnp.float32
    )
    elim[...] = corner * hess_scale + jnp.where(diagonal, damping, 0.0)
    row_number = lax.broadcasted_iota(jnp.int32, (PANEL, 1), 0)
    lane_number = lax.broadcasted_iota(jnp.int32, (1, PANEL), 1)

    def eliminate(number, carry):
        j = GROUP * number
        group = range(GROUP)
        rest = elim[...]
        rows = [elim[pl.ds(j + m, 1), :] for m in group]
        lanes = [lane_number == j + m for m in group]
        below = row_number > j + GROUP - 1

        def pick(values, m):
            return jnp.sum(jnp.where(lanes[m], values, 0.0), axis=1, keepdims=True)

        cross = {(m, k): pick(rows[m], k) for m in group for k in range(m, GROUP)}
        columns = [jnp.where(below, pick(rest, m), 0.0) for m in group]
        factors = []
        for m in group:
            scale = 1.0 / cross[m, m]
            factors.append(columns[m] * scale)
            for k in range(m + 1, GROUP):
                ratio = cross[m, k] * scale
                columns[k] = columns[k] - factors[m] * cross[m, k]
                rows[k] = jnp.where(lanes[m], -ratio, rows[k] - ratio * rows[m])
                for q in range(k, GROUP):
                    cross[k, q] = cross[k, q] - ratio * cross[m, q]
        inside = jnp.logical_and(lane_number >= j, lane_number < j + GROUP)
        updated = jnp.where(jnp.logical_and(inside, below), 0.0, rest)
        for m in group:
            later = jnp.logical_and(inside, lane_number > j + m)
            taken = jnp.where(lanes[m], 1.0, jnp.where(later, 0.0, rows[m]))
            updated = updated - factors[m] * taken
        elim[...] = updated
        for m in range(1, GROUP):
            elim[pl.ds(j + m, 1), :] = rows[m]
        return carry

    groups = PANEL // GROUP
    first = 0
    for step in range(1, pair_count):
        last = groups if step == pair_count - 1 else min(groups, 14 * step - 8)
        lax.fori_loop(first, last, eliminate, 0)
        first = last
        if step < pair_count - 1:
            receive(step)
            each_send(step + 1, lambda copy: copy.start())
    done = elim[...]
    pivots = jnp.sum(jnp.where(diagonal, done, 0.0), axis=1, keepdims=True)
    inverse = jnp.where(row_ids > column_ids, done, jnp.where(diagonal, 1.0, 0.0))
    inverse = inverse * lax.rsqrt(pivots)

    receive(pair_count - 1)
    start, offset = window_of(place, share)
    hess_buf[...] = (
        lax.dot_general(
            hidden_all[:, pl.ds(pl.multiple_of(start, 128), window)],
            hidden_all[...],
            (((0,), (0,)), ((), ())),
            preferred_element_type=jnp.float32,
        )
        * hess_scale
    )
    my_rows = pl.ds(pl.multiple_of(offset, 8), share)
    store_hessian = pltpu.make_async_copy(
        hess_buf.at[my_rows, :], hessian_hbm.at[0], store_sem.at[CHUNKS]
    )
    store_hessian.start()
    own_ids = place * share + lax.broadcasted_iota(jnp.int32, (share, PANEL), 0)
    own_columns = lax.broadcasted_iota(jnp.int32, (share, PANEL), 1)
    leading = hess_buf[my_rows, 0:PANEL] + jnp.where(own_ids == own_columns, damping, 0.0)
    panel_buf[...] = lax.dot_general(
        leading,
        inverse,
        (((1,), (1,)), ((), ())),
        precision=HIGHEST,
        preferred_element_type=jnp.float32,
    )
    store_panel = pltpu.make_async_copy(panel_buf, panel_hbm.at[0], store_sem.at[CHUNKS + 1])
    store_panel.start()

    for c in range(CHUNKS):
        for i in range(1, owners):
            back(c, i).wait_recv()
        keep(c).wait()
    for c in range(CHUNKS):
        for i in range(1, owners):
            there(c, i).wait_send()
            back(c, i).wait_send()
    for i in range(1, pair_count):
        for kind in range(2):
            shared(kind, i).wait_send()
    store_hessian.wait()
    for step in range(1, pair_count):
        each_send(step, lambda copy: copy.wait_send())
    store_panel.wait()
    store_mix.wait()


def combine(
    returned,
    mix_ref,
    hessian_hbm,
    panel_hbm,
    combined_hbm,
    hessian_out,
    panel_out,
    rows_buf,
    mixed,
    load_sem,
    store_sem,
    pass_sem,
):
    width = returned.shape[2]

    def load(c):
        return pltpu.make_async_copy(returned.at[c], rows_buf.at[c], load_sem.at[c])

    def store(c):
        cols = pl.ds(c * width, width)
        return pltpu.make_async_copy(mixed.at[c], combined_hbm.at[:, cols], store_sem.at[c])

    passes = (
        pltpu.make_async_copy(hessian_hbm, hessian_out, pass_sem.at[0]),
        pltpu.make_async_copy(panel_hbm, panel_out, pass_sem.at[1]),
    )
    for c in range(CHUNKS):
        load(c).start()
    for copy in passes:
        copy.start()
    for c in range(CHUNKS):
        load(c).wait()
        rows = rows_buf[c]
        mixed[c] = (
            jnp.dot(mix_ref[0], rows, preferred_element_type=jnp.float32)
            + jnp.dot(mix_ref[1], rows, preferred_element_type=jnp.float32)
        ).astype(jnp.bfloat16)
        store(c).start()
    for c in range(CHUNKS):
        store(c).wait()
    for copy in passes:
        copy.wait()


def per_device(
    owners, pair_count, tokens, expert_ids, route_weight, gate_weight, up_weight, down_weight
):
    tok_count, model_width = tokens.shape
    width = model_width // CHUNKS
    slots = owners * CAP
    share = FF // pair_count
    reach = max(window_of(p, share)[1] for p in range(pair_count)) + share
    window = -(-reach // 128) * 128
    vmem = pl.BlockSpec(memory_space=pltpu.VMEM)
    hbm = pl.BlockSpec(memory_space=pl.ANY)
    bf16, f32 = jnp.bfloat16, jnp.float32
    dma = pltpu.SemaphoreType.DMA
    returned, mix, hessian, panel = pl.pallas_call(
        functools.partial(kernel, owners, pair_count, window),
        out_shape=(
            jax.ShapeDtypeStruct((CHUNKS, slots, width), bf16),
            jax.ShapeDtypeStruct((2, tok_count, slots), bf16),
            jax.ShapeDtypeStruct((1, share, FF), f32),
            jax.ShapeDtypeStruct((1, share, PANEL), f32),
        ),
        in_specs=[vmem, vmem, vmem, hbm, hbm, hbm],
        out_specs=(hbm, hbm, hbm, hbm),
        scratch_shapes=[
            pltpu.VMEM((CHUNKS, width, FF), bf16),
            pltpu.VMEM((CHUNKS, width, FF), bf16),
            pltpu.VMEM((CHUNKS, FF, width), bf16),
            pltpu.VMEM((CHUNKS, slots, width), bf16),
            pltpu.VMEM((CHUNKS, slots, width), bf16),
            pltpu.VMEM((CHUNKS, slots, width), bf16),
            pltpu.VMEM((2, tok_count, slots), bf16),
            pltpu.VMEM((slots, FF), f32),
            pltpu.VMEM((slots, FF), f32),
            pltpu.VMEM((pair_count * slots, FF), bf16),
            pltpu.VMEM((pair_count, 8, 128), f32),
            pltpu.VMEM((PANEL, PANEL), f32),
            pltpu.VMEM((window, FF), f32),
            pltpu.VMEM((share, PANEL), f32),
            dma((3, CHUNKS)),
            dma((CHUNKS, owners - 1)),
            dma((CHUNKS, owners - 1)),
            dma((CHUNKS, owners - 1)),
            dma((CHUNKS, owners - 1)),
            dma((2, pair_count - 1)),
            dma((2, pair_count - 1)),
            dma((2, pair_count - 1)),
            dma((2, pair_count - 1)),
            dma((CHUNKS + 3,)),
        ],
        compiler_params=pltpu.CompilerParams(
            collective_id=0, has_side_effects=True, vmem_limit_bytes=56 * 1024 * 1024
        ),
        cost_estimate=pl.CostEstimate(
            flops=2 * slots * model_width * FF * 3,
            bytes_accessed=3 * 2 * model_width * FF,
            transcendentals=slots * FF,
        ),
        name="experts",
    )(tokens, expert_ids.T, route_weight.T, gate_weight, up_weight, down_weight)
    return pl.pallas_call(
        combine,
        out_shape=(
            jax.ShapeDtypeStruct((tok_count, model_width), bf16),
            jax.ShapeDtypeStruct((1, share, FF), f32),
            jax.ShapeDtypeStruct((1, share, PANEL), f32),
        ),
        in_specs=[hbm, vmem, hbm, hbm],
        out_specs=(hbm, hbm, hbm),
        scratch_shapes=[
            pltpu.VMEM((CHUNKS, slots, width), bf16),
            pltpu.VMEM((CHUNKS, tok_count, width), bf16),
            dma((CHUNKS,)),
            dma((CHUNKS,)),
            dma((2,)),
        ],
        compiler_params=pltpu.CompilerParams(vmem_limit_bytes=48 * 1024 * 1024),
        cost_estimate=pl.CostEstimate(
            flops=4 * tok_count * slots * model_width,
            bytes_accessed=4 * slots * model_width + 8 * share * (FF + PANEL),
            transcendentals=0,
        ),
        name="combine",
    )(returned, mix, hessian, panel)


def solution(mesh):
    in_specs = (
        P(("expert", "pair"), None),
        P(("expert", "pair"), None),
        P(("expert", "pair"), None),
        P("expert", None, None),
        P("expert", None, None),
        P("expert", None, None),
    )
    out_specs = (P(("expert", "pair"), None), P("expert", "pair", None), P("expert", "pair", None))
    return jax.shard_map(
        functools.partial(per_device, mesh.shape["expert"], mesh.shape["pair"]),
        mesh=mesh,
        in_specs=in_specs,
        out_specs=out_specs,
        check_vma=False,
    )
```

```python
import functools

import jax
import jax.numpy as jnp
from jax import lax
from jax.experimental import pallas as pl
from jax.experimental.pallas import tpu as pltpu
from jax.sharding import PartitionSpec as P

EXPERTS = 128
FF = 768
PANEL = 128
CAP = 16
CHUNKS = 4
GROUP = 4
MESH = pl.DeviceIdType.MESH
HIGHEST = lax.Precision.HIGHEST


def window_of(place, share):
    start = (place * share) // 128 * 128
    return start, place * share - start


def kernel(
    owners,
    pair_count,
    window,
    tokens_ref,
    ids_ref,
    weight_ref,
    gate_hbm,
    up_hbm,
    down_hbm,
    returned,
    mix_hbm,
    hessian_hbm,
    panel_hbm,
    gate_buf,
    up_buf,
    down_buf,
    outgoing,
    arrived,
    results,
    mix_buf,
    gate_acc,
    up_acc,
    hidden_all,
    squares,
    elim,
    hess_buf,
    panel_buf,
    load_sem,
    there_send,
    there_recv,
    back_send,
    back_recv,
    pair_send,
    pair_recv,
    pass_send,
    pass_recv,
    store_sem,
):
    me = lax.axis_index("expert")
    place = lax.axis_index("pair")
    tok_count, model_width = tokens_ref.shape
    width = model_width // CHUNKS
    slots = owners * CAP
    per_owner = EXPERTS // owners
    share = FF // pair_count
    hess_scale = 2.0 / (CAP * owners * pair_count)

    def load(kind, c):
        cols = pl.ds(pl.multiple_of(c * width, 128), width)
        source, target = (
            (gate_hbm.at[0, cols, :], gate_buf.at[c]),
            (up_hbm.at[0, cols, :], up_buf.at[c]),
            (down_hbm.at[0, :, cols], down_buf.at[c]),
        )[kind]
        return pltpu.make_async_copy(source, target, load_sem.at[kind, c])

    for c in range(CHUNKS):
        load(0, c).start()
        load(1, c).start()
    for c in range(CHUNKS):
        load(2, c).start()

    barrier = pltpu.get_barrier_semaphore()
    for i in range(1, owners):
        pl.semaphore_signal(
            barrier, inc=1, device_id=(lax.rem(me + i, owners), place), device_id_type=MESH
        )
    for i in range(1, pair_count):
        pl.semaphore_signal(
            barrier, inc=1, device_id=(me, lax.rem(place + i, pair_count)), device_id_type=MESH
        )

    slot = lax.broadcasted_iota(jnp.int32, (slots, tok_count), 0)
    target = (slot // CAP) * per_owner
    picked = jnp.zeros((slots, tok_count), jnp.float32)
    slot_weight = jnp.zeros((slots, tok_count), jnp.float32)
    for k in range(ids_ref.shape[0]):
        hit = ids_ref[k : k + 1, :] == target
        picked = jnp.where(hit, 1.0, picked)
        slot_weight = jnp.where(hit, weight_ref[k : k + 1, :], slot_weight)
    earlier = lax.broadcasted_iota(jnp.int32, (tok_count, tok_count), 0) < lax.broadcasted_iota(
        jnp.int32, (tok_count, tok_count), 1
    )
    before = jnp.dot(
        picked.astype(jnp.bfloat16),
        earlier.astype(jnp.float32).astype(jnp.bfloat16),
        preferred_element_type=jnp.float32,
    )
    rank = (slot % CAP).astype(jnp.float32)
    marks = jnp.where(before == rank, picked, 0.0)
    marks_by_slot = marks.astype(jnp.bfloat16)

    pl.semaphore_wait(barrier, owners + pair_count - 2)

    def there(c, i):
        peer = lax.rem(me + i, owners)
        return pltpu.make_async_remote_copy(
            src_ref=outgoing.at[c, pl.ds(pl.multiple_of(peer * CAP, CAP), CAP), :],
            dst_ref=arrived.at[c, pl.ds(pl.multiple_of(me * CAP, CAP), CAP), :],
            send_sem=there_send.at[c, i - 1],
            recv_sem=there_recv.at[c, i - 1],
            device_id=(peer, place),
            device_id_type=MESH,
        )

    def back(c, i):
        peer = lax.rem(me + i, owners)
        return pltpu.make_async_remote_copy(
            src_ref=results.at[c, pl.ds(pl.multiple_of(peer * CAP, CAP), CAP), :],
            dst_ref=returned.at[c, pl.ds(pl.multiple_of(me * CAP, CAP), CAP), :],
            send_sem=back_send.at[c, i - 1],
            recv_sem=back_recv.at[c, i - 1],
            device_id=(peer, place),
            device_id_type=MESH,
        )

    def keep(c):
        return pltpu.make_async_copy(
            results.at[c, mine, :], returned.at[c, mine, :], store_sem.at[c]
        )

    mine = pl.ds(pl.multiple_of(me * CAP, CAP), CAP)

    for c in range(CHUNKS):
        outgoing[c] = jnp.dot(
            marks_by_slot,
            tokens_ref[:, c * width : (c + 1) * width],
            preferred_element_type=jnp.float32,
        ).astype(jnp.bfloat16)
        for i in range(1, owners):
            there(c, i).start()
        arrived[c, mine, :] = outgoing[c, mine, :]

    weights = (slot_weight * marks).T
    weight_high = weights.astype(jnp.bfloat16)
    mix_buf[0] = weight_high
    mix_buf[1] = (weights - weight_high.astype(jnp.float32)).astype(jnp.bfloat16)
    store_mix = pltpu.make_async_copy(mix_buf, mix_hbm, store_sem.at[CHUNKS + 2])
    store_mix.start()

    gate_acc[...] = jnp.zeros_like(gate_acc)
    up_acc[...] = jnp.zeros_like(up_acc)

    def project(c, carry):
        load(0, c).wait()
        load(1, c).wait()
        for i in range(1, owners):
            there(c, i).wait_recv()
        rows = arrived[c]
        gate_acc[...] += jnp.dot(rows, gate_buf[c], preferred_element_type=jnp.float32)
        up_acc[...] += jnp.dot(rows, up_buf[c], preferred_element_type=jnp.float32)
        return carry

    lax.fori_loop(0, CHUNKS, project, 0)

    gate = gate_acc[...]
    hidden = (gate / (1.0 + jnp.exp(-gate)) * up_acc[...]).astype(jnp.bfloat16)
    block = pl.ds(pl.multiple_of(place * slots, CAP), slots)
    hidden_all[block, :] = hidden
    square = hidden.astype(jnp.float32)
    square = jnp.sum((square * square).reshape(slots // 8, 8, FF), axis=0)
    total = square[:, 0:128]
    for part in range(1, FF // 128):
        total = total + square[:, part * 128 : (part + 1) * 128]
    squares[place] = total

    def shared(kind, i):
        ref = (
            hidden_all.at[block, 0:PANEL],
            squares.at[place],
        )[kind]
        return pltpu.make_async_remote_copy(
            src_ref=ref,
            dst_ref=ref,
            send_sem=pair_send.at[kind, i - 1],
            recv_sem=pair_recv.at[kind, i - 1],
            device_id=(me, lax.rem(place + i, pair_count)),
            device_id_type=MESH,
        )

    def passing(step, side, number):
        toward = (1, -1)[side]
        ref = hidden_all.at[pl.ds(pl.multiple_of(number * slots, CAP), slots), PANEL:FF]
        return pltpu.make_async_remote_copy(
            src_ref=ref,
            dst_ref=ref,
            send_sem=pass_send.at[side, step - 1],
            recv_sem=pass_recv.at[side, step - 1],
            device_id=(me, lax.rem(place + toward + pair_count, pair_count)),
            device_id_type=MESH,
        )

    def each_send(step, action):
        @pl.when(jnp.logical_and(place >= step - 1, place < pair_count - 1))
        def _():
            action(passing(step, 0, place - step + 1))

        @pl.when(jnp.logical_and(place <= pair_count - step, place > 0))
        def _():
            action(passing(step, 1, place + step - 1))

    def receive(step):
        @pl.when(place >= step)
        def _():
            passing(step, 0, place - step).wait_recv()

        @pl.when(place < pair_count - step)
        def _():
            passing(step, 1, place + step).wait_recv()

    for kind in range(2):
        for i in range(1, pair_count):
            shared(kind, i).start()
    each_send(1, lambda copy: copy.start())

    def project_down(c, carry):
        load(2, c).wait()
        results[c] = jnp.dot(
            hidden_all[block, :], down_buf[c], preferred_element_type=jnp.float32
        ).astype(jnp.bfloat16)
        for i in range(1, owners):
            back(c, i).start()
        keep(c).start()
        return carry

    lax.fori_loop(0, CHUNKS, project_down, 0)

    for i in range(1, pair_count):
        shared(0, i).wait_recv()
        shared(1, i).wait_recv()
    damping = jnp.sum(jnp.sum(squares[...], axis=0), axis=0, keepdims=True)
    damping = jnp.sum(damping, axis=1, keepdims=True) * (0.01 * hess_scale / FF)
    row_ids = lax.broadcasted_iota(jnp.int32, (PANEL, PANEL), 0)
    column_ids = lax.broadcasted_iota(jnp.int32, (PANEL, PANEL), 1)
    diagonal = row_ids == column_ids
    lead = hidden_all[:, 0:PANEL]
    corner = lax.dot_general(
        lead, lead, (((0,), (0,)), ((), ())), preferred_element_type=jnp.float32
    )
    elim[...] = corner * hess_scale + jnp.where(diagonal, damping, 0.0)
    row_number = lax.broadcasted_iota(jnp.int32, (PANEL, 1), 0)
    lane_number = lax.broadcasted_iota(jnp.int32, (1, PANEL), 1)

    def eliminate(number, carry):
        j = GROUP * number
        group = range(GROUP)
        rest = elim[...]
        rows = [elim[pl.ds(j + m, 1), :] for m in group]
        lanes = [lane_number == j + m for m in group]
        below = row_number > j + GROUP - 1

        def pick(values, m):
            return jnp.sum(jnp.where(lanes[m], values, 0.0), axis=1, keepdims=True)

        cross = {(m, k): pick(rows[m], k) for m in group for k in range(m, GROUP)}
        columns = [jnp.where(below, pick(rest, m), 0.0) for m in group]
        factors = []
        for m in group:
            scale = 1.0 / cross[m, m]
            factors.append(columns[m] * scale)
            for k in range(m + 1, GROUP):
                ratio = cross[m, k] * scale
                columns[k] = columns[k] - factors[m] * cross[m, k]
                rows[k] = jnp.where(lanes[m], -ratio, rows[k] - ratio * rows[m])
                for q in range(k, GROUP):
                    cross[k, q] = cross[k, q] - ratio * cross[m, q]
        inside = jnp.logical_and(lane_number >= j, lane_number < j + GROUP)
        updated = jnp.where(jnp.logical_and(inside, below), 0.0, rest)
        for m in group:
            later = jnp.logical_and(inside, lane_number > j + m)
            taken = jnp.where(lanes[m], 1.0, jnp.where(later, 0.0, rows[m]))
            updated = updated - factors[m] * taken
        elim[...] = updated
        for m in range(1, GROUP):
            elim[pl.ds(j + m, 1), :] = rows[m]
        return carry

    start, offset = window_of(place, share)

    def partial(number):
        rows = pl.ds(pl.multiple_of(number * slots, CAP), slots)
        product = lax.dot_general(
            hidden_all[rows, pl.ds(pl.multiple_of(start, 128), window)],
            hidden_all[rows, :],
            (((0,), (0,)), ((), ())),
            preferred_element_type=jnp.float32,
        )
        return product * hess_scale

    def add_received(step):
        @pl.when(place >= step)
        def _():
            hess_buf[...] += partial(place - step)

        @pl.when(place < pair_count - step)
        def _():
            hess_buf[...] += partial(place + step)

    hess_buf[...] = partial(place)
    groups = PANEL // GROUP
    first = 0
    for step in range(1, pair_count):
        last = groups if step == pair_count - 1 else min(groups, 14 * step - 8)
        lax.fori_loop(first, last, eliminate, 0)
        first = last
        if step < pair_count - 1:
            receive(step)
            each_send(step + 1, lambda copy: copy.start())
            add_received(step)
    done = elim[...]
    pivots = jnp.sum(jnp.where(diagonal, done, 0.0), axis=1, keepdims=True)
    inverse = jnp.where(row_ids > column_ids, done, jnp.where(diagonal, 1.0, 0.0))
    inverse = inverse * lax.rsqrt(pivots)

    receive(pair_count - 1)
    add_received(pair_count - 1)
    my_rows = pl.ds(pl.multiple_of(offset, 8), share)
    store_hessian = pltpu.make_async_copy(
        hess_buf.at[my_rows, :], hessian_hbm.at[0], store_sem.at[CHUNKS]
    )
    store_hessian.start()
    own_ids = place * share + lax.broadcasted_iota(jnp.int32, (share, PANEL), 0)
    own_columns = lax.broadcasted_iota(jnp.int32, (share, PANEL), 1)
    leading = hess_buf[my_rows, 0:PANEL] + jnp.where(own_ids == own_columns, damping, 0.0)
    panel_buf[...] = lax.dot_general(
        leading,
        inverse,
        (((1,), (1,)), ((), ())),
        precision=HIGHEST,
        preferred_element_type=jnp.float32,
    )
    store_panel = pltpu.make_async_copy(panel_buf, panel_hbm.at[0], store_sem.at[CHUNKS + 1])
    store_panel.start()

    for c in range(CHUNKS):
        for i in range(1, owners):
            back(c, i).wait_recv()
        keep(c).wait()
    for c in range(CHUNKS):
        for i in range(1, owners):
            there(c, i).wait_send()
            back(c, i).wait_send()
    for i in range(1, pair_count):
        for kind in range(2):
            shared(kind, i).wait_send()
    store_hessian.wait()
    for step in range(1, pair_count):
        each_send(step, lambda copy: copy.wait_send())
    store_panel.wait()
    store_mix.wait()


def combine(returned_ref, mix_ref, hessian_ref, panel_ref, combined_ref, hessian_out, panel_out):
    rows = returned_ref[0]
    combined_ref[...] = (
        jnp.dot(mix_ref[0], rows, preferred_element_type=jnp.float32)
        + jnp.dot(mix_ref[1], rows, preferred_element_type=jnp.float32)
    ).astype(jnp.bfloat16)
    hessian_out[...] = hessian_ref[...]
    panel_out[...] = panel_ref[...]


def per_device(
    owners, pair_count, tokens, expert_ids, route_weight, gate_weight, up_weight, down_weight
):
    tok_count, model_width = tokens.shape
    width = model_width // CHUNKS
    slots = owners * CAP
    share = FF // pair_count
    reach = max(window_of(p, share)[1] for p in range(pair_count)) + share
    window = -(-reach // 128) * 128
    vmem = pl.BlockSpec(memory_space=pltpu.VMEM)
    hbm = pl.BlockSpec(memory_space=pl.ANY)
    bf16, f32 = jnp.bfloat16, jnp.float32
    dma = pltpu.SemaphoreType.DMA
    returned, mix, hessian, panel = pl.pallas_call(
        functools.partial(kernel, owners, pair_count, window),
        out_shape=(
            jax.ShapeDtypeStruct((CHUNKS, slots, width), bf16),
            jax.ShapeDtypeStruct((2, tok_count, slots), bf16),
            jax.ShapeDtypeStruct((1, share, FF), f32),
            jax.ShapeDtypeStruct((1, share, PANEL), f32),
        ),
        in_specs=[vmem, vmem, vmem, hbm, hbm, hbm],
        out_specs=(hbm, hbm, hbm, hbm),
        scratch_shapes=[
            pltpu.VMEM((CHUNKS, width, FF), bf16),
            pltpu.VMEM((CHUNKS, width, FF), bf16),
            pltpu.VMEM((CHUNKS, FF, width), bf16),
            pltpu.VMEM((CHUNKS, slots, width), bf16),
            pltpu.VMEM((CHUNKS, slots, width), bf16),
            pltpu.VMEM((CHUNKS, slots, width), bf16),
            pltpu.VMEM((2, tok_count, slots), bf16),
            pltpu.VMEM((slots, FF), f32),
            pltpu.VMEM((slots, FF), f32),
            pltpu.VMEM((pair_count * slots, FF), bf16),
            pltpu.VMEM((pair_count, 8, 128), f32),
            pltpu.VMEM((PANEL, PANEL), f32),
            pltpu.VMEM((window, FF), f32),
            pltpu.VMEM((share, PANEL), f32),
            dma((3, CHUNKS)),
            dma((CHUNKS, owners - 1)),
            dma((CHUNKS, owners - 1)),
            dma((CHUNKS, owners - 1)),
            dma((CHUNKS, owners - 1)),
            dma((2, pair_count - 1)),
            dma((2, pair_count - 1)),
            dma((2, pair_count - 1)),
            dma((2, pair_count - 1)),
            dma((CHUNKS + 3,)),
        ],
        compiler_params=pltpu.CompilerParams(
            collective_id=0, has_side_effects=True, vmem_limit_bytes=56 * 1024 * 1024
        ),
        cost_estimate=pl.CostEstimate(
            flops=2 * slots * model_width * FF * 3,
            bytes_accessed=3 * 2 * model_width * FF,
            transcendentals=slots * FF,
        ),
        name="experts",
    )(tokens, expert_ids.T, route_weight.T, gate_weight, up_weight, down_weight)
    strip = share // CHUNKS
    hessian_spec = pl.BlockSpec((1, strip, FF), lambda c: (0, c, 0))
    panel_spec = pl.BlockSpec((1, strip, PANEL), lambda c: (0, c, 0))
    return pl.pallas_call(
        combine,
        grid=(CHUNKS,),
        out_shape=(
            jax.ShapeDtypeStruct((tok_count, model_width), bf16),
            jax.ShapeDtypeStruct((1, share, FF), f32),
            jax.ShapeDtypeStruct((1, share, PANEL), f32),
        ),
        in_specs=[
            pl.BlockSpec((1, slots, width), lambda c: (c, 0, 0)),
            pl.BlockSpec((2, tok_count, slots), lambda c: (0, 0, 0)),
            hessian_spec,
            panel_spec,
        ],
        out_specs=(
            pl.BlockSpec((tok_count, width), lambda c: (0, c)),
            hessian_spec,
            panel_spec,
        ),
        cost_estimate=pl.CostEstimate(
            flops=4 * tok_count * slots * model_width,
            bytes_accessed=4 * slots * model_width + 8 * share * (FF + PANEL),
            transcendentals=0,
        ),
        name="combine",
    )(returned, mix, hessian, panel)


def solution(mesh):
    in_specs = (
        P(("expert", "pair"), None),
        P(("expert", "pair"), None),
        P(("expert", "pair"), None),
        P("expert", None, None),
        P("expert", None, None),
        P("expert", None, None),
    )
    out_specs = (P(("expert", "pair"), None), P("expert", "pair", None), P("expert", "pair", None))
    return jax.shard_map(
        functools.partial(per_device, mesh.shape["expert"], mesh.shape["pair"]),
        mesh=mesh,
        in_specs=in_specs,
        out_specs=out_specs,
        check_vma=False,
    )
```

```python
import functools

import jax
import jax.numpy as jnp
from jax import lax
from jax.experimental import pallas as pl
from jax.experimental.pallas import tpu as pltpu
from jax.sharding import PartitionSpec as P

EXPERTS = 128
FF = 768
PANEL = 128
CAP = 16
CHUNKS = 4
STEPS = 2
GROUP = 4
MESH = pl.DeviceIdType.MESH
HIGHEST = lax.Precision.HIGHEST


def window_of(place, share):
    start = (place * share) // 128 * 128
    return start, place * share - start


def kernel(
    owners,
    pair_count,
    window,
    tokens_ref,
    ids_ref,
    weight_ref,
    gate_hbm,
    up_hbm,
    down_hbm,
    returned,
    mix_hbm,
    hessian_hbm,
    panel_hbm,
    gate_buf,
    up_buf,
    down_buf,
    outgoing,
    arrived,
    results,
    mix_buf,
    gate_acc,
    up_acc,
    hidden_all,
    squares,
    elim,
    hess_buf,
    panel_buf,
    load_sem,
    there_send,
    there_recv,
    back_send,
    back_recv,
    pair_send,
    pair_recv,
    pass_send,
    pass_recv,
    store_sem,
):
    me = lax.axis_index("expert")
    place = lax.axis_index("pair")
    tok_count, model_width = tokens_ref.shape
    width = model_width // CHUNKS
    slots = owners * CAP
    per_owner = EXPERTS // owners
    share = FF // pair_count
    hess_scale = 2.0 / (CAP * owners * pair_count)

    def load(kind, c):
        cols = pl.ds(pl.multiple_of(c * width, 128), width)
        source, target = (
            (gate_hbm.at[0, cols, :], gate_buf.at[c]),
            (up_hbm.at[0, cols, :], up_buf.at[c]),
            (down_hbm.at[0, :, cols], down_buf.at[c]),
        )[kind]
        return pltpu.make_async_copy(source, target, load_sem.at[kind, c])

    for c in range(CHUNKS):
        load(0, c).start()
        load(1, c).start()
    for c in range(CHUNKS):
        load(2, c).start()

    barrier = pltpu.get_barrier_semaphore()
    for i in range(1, owners):
        pl.semaphore_signal(
            barrier, inc=1, device_id=(lax.rem(me + i, owners), place), device_id_type=MESH
        )
    for i in range(1, pair_count):
        pl.semaphore_signal(
            barrier, inc=1, device_id=(me, lax.rem(place + i, pair_count)), device_id_type=MESH
        )

    slot = lax.broadcasted_iota(jnp.int32, (slots, tok_count), 0)
    target = (slot // CAP) * per_owner
    picked = jnp.zeros((slots, tok_count), jnp.float32)
    slot_weight = jnp.zeros((slots, tok_count), jnp.float32)
    for k in range(ids_ref.shape[0]):
        hit = ids_ref[k : k + 1, :] == target
        picked = jnp.where(hit, 1.0, picked)
        slot_weight = jnp.where(hit, weight_ref[k : k + 1, :], slot_weight)
    earlier = lax.broadcasted_iota(jnp.int32, (tok_count, tok_count), 0) < lax.broadcasted_iota(
        jnp.int32, (tok_count, tok_count), 1
    )
    before = jnp.dot(
        picked.astype(jnp.bfloat16),
        earlier.astype(jnp.float32).astype(jnp.bfloat16),
        preferred_element_type=jnp.float32,
    )
    rank = (slot % CAP).astype(jnp.float32)
    marks = jnp.where(before == rank, picked, 0.0)
    marks_by_slot = marks.astype(jnp.bfloat16)

    pl.semaphore_wait(barrier, owners + pair_count - 2)

    def there(c, i):
        peer = lax.rem(me + i, owners)
        return pltpu.make_async_remote_copy(
            src_ref=outgoing.at[c, pl.ds(pl.multiple_of(peer * CAP, CAP), CAP), :],
            dst_ref=arrived.at[c, pl.ds(pl.multiple_of(me * CAP, CAP), CAP), :],
            send_sem=there_send.at[c, i - 1],
            recv_sem=there_recv.at[c, i - 1],
            device_id=(peer, place),
            device_id_type=MESH,
        )

    def back(c, i):
        peer = lax.rem(me + i, owners)
        return pltpu.make_async_remote_copy(
            src_ref=results.at[c, pl.ds(pl.multiple_of(peer * CAP, CAP), CAP), :],
            dst_ref=returned.at[c, pl.ds(pl.multiple_of(me * CAP, CAP), CAP), :],
            send_sem=back_send.at[c, i - 1],
            recv_sem=back_recv.at[c, i - 1],
            device_id=(peer, place),
            device_id_type=MESH,
        )

    def keep(c):
        return pltpu.make_async_copy(
            results.at[c, mine, :], returned.at[c, mine, :], store_sem.at[c]
        )

    mine = pl.ds(pl.multiple_of(me * CAP, CAP), CAP)

    for c in range(CHUNKS):
        outgoing[c] = jnp.dot(
            marks_by_slot,
            tokens_ref[:, c * width : (c + 1) * width],
            preferred_element_type=jnp.float32,
        ).astype(jnp.bfloat16)
        for i in range(1, owners):
            there(c, i).start()
        arrived[c, mine, :] = outgoing[c, mine, :]

    weights = (slot_weight * marks).T
    weight_high = weights.astype(jnp.bfloat16)
    mix_buf[0] = weight_high
    mix_buf[1] = (weights - weight_high.astype(jnp.float32)).astype(jnp.bfloat16)
    store_mix = pltpu.make_async_copy(mix_buf, mix_hbm, store_sem.at[CHUNKS + 2])
    store_mix.start()

    gate_acc[...] = jnp.zeros_like(gate_acc)
    up_acc[...] = jnp.zeros_like(up_acc)

    def project(c, carry):
        load(0, c).wait()
        load(1, c).wait()
        for i in range(1, owners):
            there(c, i).wait_recv()
        rows = arrived[c]
        gate_acc[...] += jnp.dot(rows, gate_buf[c], preferred_element_type=jnp.float32)
        up_acc[...] += jnp.dot(rows, up_buf[c], preferred_element_type=jnp.float32)
        return carry

    lax.fori_loop(0, CHUNKS, project, 0)

    gate = gate_acc[...]
    hidden = (gate / (1.0 + jnp.exp(-gate)) * up_acc[...]).astype(jnp.bfloat16)
    block = pl.ds(pl.multiple_of(place * slots, CAP), slots)
    hidden_all[block, :] = hidden
    square = hidden.astype(jnp.float32)
    square = jnp.sum((square * square).reshape(slots // 8, 8, FF), axis=0)
    total = square[:, 0:128]
    for part in range(1, FF // 128):
        total = total + square[:, part * 128 : (part + 1) * 128]
    squares[place] = total

    def shared(kind, i):
        ref = (
            hidden_all.at[block, 0:PANEL],
            squares.at[place],
        )[kind]
        return pltpu.make_async_remote_copy(
            src_ref=ref,
            dst_ref=ref,
            send_sem=pair_send.at[kind, i - 1],
            recv_sem=pair_recv.at[kind, i - 1],
            device_id=(me, lax.rem(place + i, pair_count)),
            device_id_type=MESH,
        )

    def passing(step, side, number):
        toward = (1, -1)[side]
        ref = hidden_all.at[pl.ds(pl.multiple_of(number * slots, CAP), slots), PANEL:FF]
        return pltpu.make_async_remote_copy(
            src_ref=ref,
            dst_ref=ref,
            send_sem=pass_send.at[side, step - 1],
            recv_sem=pass_recv.at[side, step - 1],
            device_id=(me, lax.rem(place + toward + pair_count, pair_count)),
            device_id_type=MESH,
        )

    def each_send(step, action):
        @pl.when(jnp.logical_and(place >= step - 1, place < pair_count - 1))
        def _():
            action(passing(step, 0, place - step + 1))

        @pl.when(jnp.logical_and(place <= pair_count - step, place > 0))
        def _():
            action(passing(step, 1, place + step - 1))

    def receive(step):
        @pl.when(place >= step)
        def _():
            passing(step, 0, place - step).wait_recv()

        @pl.when(place < pair_count - step)
        def _():
            passing(step, 1, place + step).wait_recv()

    for kind in range(2):
        for i in range(1, pair_count):
            shared(kind, i).start()
    each_send(1, lambda copy: copy.start())

    def project_down(c, carry):
        load(2, c).wait()
        results[c] = jnp.dot(
            hidden_all[block, :], down_buf[c], preferred_element_type=jnp.float32
        ).astype(jnp.bfloat16)
        for i in range(1, owners):
            back(c, i).start()
        keep(c).start()
        return carry

    lax.fori_loop(0, CHUNKS, project_down, 0)

    for i in range(1, pair_count):
        shared(0, i).wait_recv()
        shared(1, i).wait_recv()
    damping = jnp.sum(jnp.sum(squares[...], axis=0), axis=0, keepdims=True)
    damping = jnp.sum(damping, axis=1, keepdims=True) * (0.01 * hess_scale / FF)
    row_ids = lax.broadcasted_iota(jnp.int32, (PANEL, PANEL), 0)
    column_ids = lax.broadcasted_iota(jnp.int32, (PANEL, PANEL), 1)
    diagonal = row_ids == column_ids
    lead = hidden_all[:, 0:PANEL]
    corner = lax.dot_general(
        lead, lead, (((0,), (0,)), ((), ())), preferred_element_type=jnp.float32
    )
    elim[...] = corner * hess_scale + jnp.where(diagonal, damping, 0.0)
    row_number = lax.broadcasted_iota(jnp.int32, (PANEL, 1), 0)
    lane_number = lax.broadcasted_iota(jnp.int32, (1, PANEL), 1)

    def eliminate(number, carry):
        j = GROUP * number
        group = range(GROUP)
        rest = elim[...]
        rows = [elim[pl.ds(j + m, 1), :] for m in group]
        lanes = [lane_number == j + m for m in group]
        below = row_number > j + GROUP - 1

        def pick(values, m):
            return jnp.sum(jnp.where(lanes[m], values, 0.0), axis=1, keepdims=True)

        cross = {(m, k): pick(rows[m], k) for m in group for k in range(m, GROUP)}
        columns = [jnp.where(below, pick(rest, m), 0.0) for m in group]
        factors = []
        for m in group:
            scale = 1.0 / cross[m, m]
            factors.append(columns[m] * scale)
            for k in range(m + 1, GROUP):
                ratio = cross[m, k] * scale
                columns[k] = columns[k] - factors[m] * cross[m, k]
                rows[k] = jnp.where(lanes[m], -ratio, rows[k] - ratio * rows[m])
                for q in range(k, GROUP):
                    cross[k, q] = cross[k, q] - ratio * cross[m, q]
        inside = jnp.logical_and(lane_number >= j, lane_number < j + GROUP)
        updated = jnp.where(jnp.logical_and(inside, below), 0.0, rest)
        for m in group:
            later = jnp.logical_and(inside, lane_number > j + m)
            taken = jnp.where(lanes[m], 1.0, jnp.where(later, 0.0, rows[m]))
            updated = updated - factors[m] * taken
        elim[...] = updated
        for m in range(1, GROUP):
            elim[pl.ds(j + m, 1), :] = rows[m]
        return carry

    start, offset = window_of(place, share)

    def partial(number):
        rows = pl.ds(pl.multiple_of(number * slots, CAP), slots)
        product = lax.dot_general(
            hidden_all[rows, pl.ds(pl.multiple_of(start, 128), window)],
            hidden_all[rows, :],
            (((0,), (0,)), ((), ())),
            preferred_element_type=jnp.float32,
        )
        return product * hess_scale

    def add_received(step):
        @pl.when(place >= step)
        def _():
            hess_buf[...] += partial(place - step)

        @pl.when(place < pair_count - step)
        def _():
            hess_buf[...] += partial(place + step)

    hess_buf[...] = partial(place)
    groups = PANEL // GROUP
    first = 0
    for step in range(1, pair_count):
        last = groups if step == pair_count - 1 else min(groups, 14 * step - 8)
        lax.fori_loop(first, last, eliminate, 0)
        first = last
        if step < pair_count - 1:
            receive(step)
            each_send(step + 1, lambda copy: copy.start())
            add_received(step)
    done = elim[...]
    pivots = jnp.sum(jnp.where(diagonal, done, 0.0), axis=1, keepdims=True)
    inverse = jnp.where(row_ids > column_ids, done, jnp.where(diagonal, 1.0, 0.0))
    inverse = inverse * lax.rsqrt(pivots)

    receive(pair_count - 1)
    add_received(pair_count - 1)
    my_rows = pl.ds(pl.multiple_of(offset, 8), share)
    store_hessian = pltpu.make_async_copy(
        hess_buf.at[my_rows, :], hessian_hbm.at[0], store_sem.at[CHUNKS]
    )
    store_hessian.start()
    own_ids = place * share + lax.broadcasted_iota(jnp.int32, (share, PANEL), 0)
    own_columns = lax.broadcasted_iota(jnp.int32, (share, PANEL), 1)
    leading = hess_buf[my_rows, 0:PANEL] + jnp.where(own_ids == own_columns, damping, 0.0)
    panel_buf[...] = lax.dot_general(
        leading,
        inverse,
        (((1,), (1,)), ((), ())),
        precision=HIGHEST,
        preferred_element_type=jnp.float32,
    )
    store_panel = pltpu.make_async_copy(panel_buf, panel_hbm.at[0], store_sem.at[CHUNKS + 1])
    store_panel.start()

    for c in range(CHUNKS):
        for i in range(1, owners):
            back(c, i).wait_recv()
        keep(c).wait()
    for c in range(CHUNKS):
        for i in range(1, owners):
            there(c, i).wait_send()
            back(c, i).wait_send()
    for i in range(1, pair_count):
        for kind in range(2):
            shared(kind, i).wait_send()
    store_hessian.wait()
    for step in range(1, pair_count):
        each_send(step, lambda copy: copy.wait_send())
    store_panel.wait()
    store_mix.wait()


def combine(returned_ref, mix_ref, hessian_ref, panel_ref, combined_ref, hessian_out, panel_out):
    width = returned_ref.shape[2]
    for c in range(returned_ref.shape[0]):
        rows = returned_ref[c]
        combined_ref[:, c * width : (c + 1) * width] = (
            jnp.dot(mix_ref[0], rows, preferred_element_type=jnp.float32)
            + jnp.dot(mix_ref[1], rows, preferred_element_type=jnp.float32)
        ).astype(jnp.bfloat16)
    hessian_out[...] = hessian_ref[...]
    panel_out[...] = panel_ref[...]


def per_device(
    owners, pair_count, tokens, expert_ids, route_weight, gate_weight, up_weight, down_weight
):
    tok_count, model_width = tokens.shape
    width = model_width // CHUNKS
    slots = owners * CAP
    share = FF // pair_count
    reach = max(window_of(p, share)[1] for p in range(pair_count)) + share
    window = -(-reach // 128) * 128
    vmem = pl.BlockSpec(memory_space=pltpu.VMEM)
    hbm = pl.BlockSpec(memory_space=pl.ANY)
    bf16, f32 = jnp.bfloat16, jnp.float32
    dma = pltpu.SemaphoreType.DMA
    returned, mix, hessian, panel = pl.pallas_call(
        functools.partial(kernel, owners, pair_count, window),
        out_shape=(
            jax.ShapeDtypeStruct((CHUNKS, slots, width), bf16),
            jax.ShapeDtypeStruct((2, tok_count, slots), bf16),
            jax.ShapeDtypeStruct((1, share, FF), f32),
            jax.ShapeDtypeStruct((1, share, PANEL), f32),
        ),
        in_specs=[vmem, vmem, vmem, hbm, hbm, hbm],
        out_specs=(hbm, hbm, hbm, hbm),
        scratch_shapes=[
            pltpu.VMEM((CHUNKS, width, FF), bf16),
            pltpu.VMEM((CHUNKS, width, FF), bf16),
            pltpu.VMEM((CHUNKS, FF, width), bf16),
            pltpu.VMEM((CHUNKS, slots, width), bf16),
            pltpu.VMEM((CHUNKS, slots, width), bf16),
            pltpu.VMEM((CHUNKS, slots, width), bf16),
            pltpu.VMEM((2, tok_count, slots), bf16),
            pltpu.VMEM((slots, FF), f32),
            pltpu.VMEM((slots, FF), f32),
            pltpu.VMEM((pair_count * slots, FF), bf16),
            pltpu.VMEM((pair_count, 8, 128), f32),
            pltpu.VMEM((PANEL, PANEL), f32),
            pltpu.VMEM((window, FF), f32),
            pltpu.VMEM((share, PANEL), f32),
            dma((3, CHUNKS)),
            dma((CHUNKS, owners - 1)),
            dma((CHUNKS, owners - 1)),
            dma((CHUNKS, owners - 1)),
            dma((CHUNKS, owners - 1)),
            dma((2, pair_count - 1)),
            dma((2, pair_count - 1)),
            dma((2, pair_count - 1)),
            dma((2, pair_count - 1)),
            dma((CHUNKS + 3,)),
        ],
        compiler_params=pltpu.CompilerParams(
            collective_id=0, has_side_effects=True, vmem_limit_bytes=56 * 1024 * 1024
        ),
        cost_estimate=pl.CostEstimate(
            flops=2 * slots * model_width * FF * 3,
            bytes_accessed=3 * 2 * model_width * FF,
            transcendentals=slots * FF,
        ),
        name="experts",
    )(tokens, expert_ids.T, route_weight.T, gate_weight, up_weight, down_weight)
    strip = share // STEPS
    per_step = CHUNKS // STEPS
    hessian_spec = pl.BlockSpec((1, strip, FF), lambda c: (0, c, 0))
    panel_spec = pl.BlockSpec((1, strip, PANEL), lambda c: (0, c, 0))
    return pl.pallas_call(
        combine,
        grid=(STEPS,),
        out_shape=(
            jax.ShapeDtypeStruct((tok_count, model_width), bf16),
            jax.ShapeDtypeStruct((1, share, FF), f32),
            jax.ShapeDtypeStruct((1, share, PANEL), f32),
        ),
        in_specs=[
            pl.BlockSpec((per_step, slots, width), lambda c: (c, 0, 0)),
            pl.BlockSpec((2, tok_count, slots), lambda c: (0, 0, 0)),
            hessian_spec,
            panel_spec,
        ],
        out_specs=(
            pl.BlockSpec((tok_count, per_step * width), lambda c: (0, c)),
            hessian_spec,
            panel_spec,
        ),
        cost_estimate=pl.CostEstimate(
            flops=4 * tok_count * slots * model_width,
            bytes_accessed=4 * slots * model_width + 8 * share * (FF + PANEL),
            transcendentals=0,
        ),
        name="combine",
    )(returned, mix, hessian, panel)


def solution(mesh):
    in_specs = (
        P(("expert", "pair"), None),
        P(("expert", "pair"), None),
        P(("expert", "pair"), None),
        P("expert", None, None),
        P("expert", None, None),
        P("expert", None, None),
    )
    out_specs = (P(("expert", "pair"), None), P("expert", "pair", None), P("expert", "pair", None))
    return jax.shard_map(
        functools.partial(per_device, mesh.shape["expert"], mesh.shape["pair"]),
        mesh=mesh,
        in_specs=in_specs,
        out_specs=out_specs,
        check_vma=False,
    )
```
